256 devices in a mesh: patch: 32 (over z, x_hi, core), head: 8 (over y, x_lo).
Axes of the slice: x: 4 (x_hi: 2, x_lo: 2; x = x_hi * 2 + x_lo), y: 4, z: 8, core: 2. Of those that a mesh axis runs over, the one named last changes fastest.
Arguments:
- queries: bfloat16 [8192, 3072], P(('patch', 'head')), may hold values from -10 to 10
- fresh_keys: bfloat16 [8192, 3072], P('patch', 'head'), may hold values from -6 to 6
- fresh_values: bfloat16 [8192, 3072], P('patch', 'head'), may hold values from -6 to 6
- stale_keys: bfloat16 [8192, 3072], P(None, 'head'), may hold values from -6 to 6
- stale_values: bfloat16 [8192, 3072], P(None, 'head'), may hold values from -6 to 6
- key_basis: bfloat16 [24, 128, 64], P('head'), may hold values from -0.5 to 0.5
- value_basis: bfloat16 [24, 128, 64], P('head'), may hold values from -0.5 to 0.5
- owner_table: int32 [32], replicated, may hold values from 0 to 31, each once
- step_counter: int32 [32], replicated, may hold values from 0 to 3
Outputs:
- attended: bfloat16 [8192, 3072], P(('patch', 'head'))
The draws below stay inside these ranges and needn't reach their ends.
Inputs may be any that keep to these rules, and one draw needn't show every extreme that they name: `owner_table`: a permutation of the patches.
All inputs are finite; a program needn't handle non-finite values.
Results may differ from the reference program's by a relative error of at most 0.0049.
The reference program's roundings to bfloat16 on the way (of `weights`) count: a program that leaves them out, or rounds other values in their place, can miss the bound.
Values may be sent and summed in bfloat16 or wider, within the bound.
A program may use at most 192 MiB of HBM per device.

```python
import jax
import jax.numpy as jnp
from jax import lax

HD = 128
RANK = 64
SEQ = 8192
HEADS = 24
N_PATCH = 32


def draw_queries(key, part):
    key = jax.random.fold_in(key, 1)
    result = jnp.clip(2.5 * jax.random.normal(key, (SEQ, HEADS * HD)), -10.0, 10.0)
    return result.astype(jnp.bfloat16)


def draw_fresh_keys(key, part):
    key = jax.random.fold_in(key, 2)
    result = jnp.clip(jax.random.normal(key, (SEQ, HEADS * HD)), -6.0, 6.0)
    return result.astype(jnp.bfloat16)


def set_ends(drawn, rng, low, top_value):
    index_at = [jax.random.randint(jax.random.fold_in(rng, axis), (), 0, length) for axis, length in enumerate(drawn.shape)]
    main_axis = drawn.shape.index(max(drawn.shape))
    neighbour = index_at[:main_axis] + [(index_at[main_axis] + 1) % drawn.shape[main_axis]] + index_at[main_axis + 1:]
    return drawn.at[tuple(index_at)].set(low).at[tuple(neighbour)].set(top_value)


def levels(key, shape, shards, smallest, high):
    level, own = 1.0, jax.random.fold_in(key, 6)
    for dim, shards_of in shards:
        steps = jnp.exp(jax.random.uniform(jax.random.fold_in(own, dim), (shards_of,), jnp.float32, smallest / len(shards), high / len(shards)))
        level = level * jnp.repeat(steps, shape[dim] // shards_of).reshape([-1 if axis == dim else 1 for axis in range(len(shape))])
    return level


def scatter_about(own_key, extent, scale, bound, pieces=(), kind=jnp.bfloat16):
    gain = levels(own_key, extent, pieces, -0.22, 0.18) if pieces else 1.0
    entries = jax.random.normal(own_key, extent, jnp.float32) * scale * gain
    return jnp.minimum(jnp.maximum(entries, -bound), bound).astype(kind)


def setup_inputs(seed: int = 0) -> dict:
    keys = jax.random.split(jax.random.key(seed), 10)
    return {
        "queries": draw_queries(jax.random.fold_in(keys[9], 71), 0),
        "fresh_keys": draw_fresh_keys(jax.random.fold_in(keys[9], 71), 0),
        "fresh_values": scatter_about(keys[2], (SEQ, HEADS * HD), 1.0, 6.0, ((0, 32), (1, 8))),
        "stale_keys": scatter_about(keys[3], (SEQ, HEADS * HD), 1.0, 6.0, ((1, 8),)),
        "stale_values": scatter_about(keys[4], (SEQ, HEADS * HD), 1.0, 6.0, ((1, 8),)),
        "key_basis": scatter_about(keys[5], (HEADS, HD, RANK), HD ** -0.5, 0.5, ((0, 8),)),
        "value_basis": scatter_about(keys[6], (HEADS, HD, RANK), HD ** -0.5, 0.5, ((0, 8),)),
        "owner_table": jax.random.permutation(keys[7], N_PATCH).astype(jnp.int32),
        "step_counter": set_ends(jax.random.randint(keys[8], (N_PATCH,), 0, 4), jax.random.fold_in(keys[8], 1), 0, 3).astype(jnp.int32),
    }


def reference(queries, fresh_keys, fresh_values, stale_keys, stale_values, key_basis, value_basis, owner_table, step_counter):
    total_rows = queries.shape[0]
    head_count = key_basis.shape[0]
    patch_rows = total_rows // N_PATCH
    width = head_count * HD
    score_scale = HD ** -0.5
    blend_rate = 1.0 - jnp.exp2(-(step_counter.astype(jnp.float32) + 1.0))
    blend_row = jnp.repeat(blend_rate, patch_rows, total_repeat_length=total_rows)

    def renew_side(fresh_rows, stale_rows, basis):
        old_rows = jnp.take(stale_rows.reshape(N_PATCH, patch_rows, width), owner_table, axis=0).reshape(total_rows, width)
        delta = (fresh_rows.astype(jnp.float32) - old_rows.astype(jnp.float32)).reshape(total_rows, head_count, HD)
        basis_wide = basis.astype(jnp.float32)
        codes = jnp.einsum('shd,hdr->shr', delta, basis_wide, precision=lax.Precision.HIGHEST).astype(jnp.bfloat16)
        grown = jnp.einsum('shr,hdr->shd', codes.astype(jnp.float32), basis_wide, precision=lax.Precision.HIGHEST)
        renewed = old_rows.astype(jnp.float32).reshape(total_rows, head_count, HD) + blend_row[:, None, None] * grown
        return renewed.astype(jnp.bfloat16)

    renewed_keys = renew_side(fresh_keys, stale_keys, key_basis)
    renewed_values = renew_side(fresh_values, stale_values, value_basis)
    fresh_key_rows = fresh_keys.reshape(total_rows, head_count, HD)
    fresh_value_rows = fresh_values.reshape(total_rows, head_count, HD)
    query_rows = queries.reshape(total_rows, head_count, HD)

    def one_patch(patch_id):
        row_start = (patch_id * patch_rows).astype(jnp.int32)
        keys_here = lax.dynamic_update_slice_in_dim(renewed_keys, lax.dynamic_slice_in_dim(fresh_key_rows, row_start, patch_rows, 0), row_start, 0)
        values_here = lax.dynamic_update_slice_in_dim(renewed_values, lax.dynamic_slice_in_dim(fresh_value_rows, row_start, patch_rows, 0), row_start, 0)
        query_block = lax.dynamic_slice_in_dim(query_rows, row_start, patch_rows, 0)
        scores = jnp.einsum('qhd,khd->hqk', query_block.astype(jnp.float32), keys_here.astype(jnp.float32)) * score_scale
        best = jnp.max(scores, axis=2, keepdims=True)
        exp_scores = jnp.exp(scores - best)
        total_sum = jnp.sum(exp_scores, axis=2)
        weights = exp_scores.astype(jnp.bfloat16)
        summed = jnp.einsum('hqk,khd->qhd', weights.astype(jnp.float32), values_here.astype(jnp.float32))
        return (summed / jnp.transpose(total_sum)[:, :, None]).astype(jnp.bfloat16)

    blocks = lax.map(one_patch, jnp.arange(N_PATCH, dtype=jnp.int32))
    return blocks.reshape(total_rows, head_count * HD)
```

```python
import functools
import math

import jax
import jax.numpy as jnp
from jax import lax
from jax.experimental import pallas as pl
from jax.experimental.pallas import tpu as pltpu
from jax.sharding import PartitionSpec as P

MESH = pl.DeviceIdType.MESH
F32 = jnp.float32
BF16 = jnp.bfloat16
LOG2E = math.log2(math.e)
LANES = 128


def across(a, b):
    return lax.dot_general(a, b, (((1,), (1,)), ((), ())), preferred_element_type=F32)


def kernel(
    dims,
    owner_ref,
    step_ref,
    queries_ref,
    fresh_k_ref,
    fresh_v_ref,
    stale_k_ref,
    stale_v_ref,
    basis_k_ref,
    basis_v_ref,
    out_ref,
    stale,
    fresh,
    basis,
    qbuf,
    codes,
    keys,
    values,
    own_keys,
    own_values,
    acc,
    best,
    part_out,
    part_stat,
    got_out,
    got_stat,
    sum_out,
    sum_stat,
    final_out,
    final_stat,
    load_sem,
    q_send,
    q_recv,
    qc_sem,
    ring_send,
    ring_recv,
    part_send,
    part_recv,
    final_send,
    final_recv,
):
    heads, nz, nh, rows = dims
    width = heads * LANES
    small = rows // nh
    per_group = LANES // small
    groups = rows // LANES
    scale = LOG2E / math.sqrt(LANES)
    half = rows // 2

    patch = lax.axis_index("patch")
    head = lax.axis_index("head")
    core = lax.rem(patch, 2)
    xh = lax.rem(patch // 2, 2)
    z = patch // 4

    def patch_of(z_, x_, c_):
        return (z_ * 2 + x_) * 2 + c_

    partner = (patch_of(z, xh, 1 - core), head)
    right = (patch_of(lax.rem(z + 1, nz), xh, core), head)
    left = (patch_of(lax.rem(z + nz - 1, nz), xh, core), head)

    def plane(t):
        tx = lax.rem(xh + t // nh, 2)
        th = lax.rem(head + lax.rem(t, nh), nh)
        return tx, th

    loads = []
    for i, src in enumerate((fresh_k_ref, fresh_v_ref)):
        loads.append(pltpu.make_async_copy(src, fresh.at[i], load_sem.at[i]))
    for j in range(heads):
        for i, src in enumerate((stale_k_ref, stale_v_ref)):
            loads.append(
                pltpu.make_async_copy(
                    src.at[:, :, j * LANES : (j + 1) * LANES],
                    stale[2 * j + i],
                    load_sem.at[2 + 2 * j + i],
                )
            )
    for load in loads:
        load.start()

    barrier = pltpu.get_barrier_semaphore()
    for device in (partner, right, left):
        pl.semaphore_signal(barrier, inc=1, device_id=device, device_id_type=MESH)

    @pl.loop(1, 2 * nh)
    def _(t):
        tx, th = plane(t)
        pl.semaphore_signal(
            barrier, inc=1, device_id=(patch_of(z, tx, core), th), device_id_type=MESH
        )

    rank = basis_k_ref.shape[1]
    blank = jnp.zeros((rank, LANES), BF16)
    for j in range(heads):
        basis[j, :rank, :LANES] = basis_k_ref[j]
        basis[j, :rank, LANES:] = blank
        basis[j, rank:, :LANES] = blank
        basis[j, rank:, LANES:] = basis_v_ref[j]
    ones = jnp.ones(values.shape[:3] + (LANES,), BF16)
    values[:, :, :, LANES:] = ones
    own_values[:, :, LANES:] = ones[:, 0]
    sum_stat[...] = jnp.zeros(sum_stat.shape, F32)

    pl.semaphore_wait(barrier, 3 + 2 * nh - 1)

    def q_copy(t):
        tx, th = plane(t)
        return pltpu.make_async_remote_copy(
            src_ref=queries_ref.at[:, pl.ds(pl.multiple_of(th * width, LANES), width)],
            dst_ref=qbuf.at[
                pl.ds(pl.multiple_of((t // nh) * rows + head * small, small), small), :
            ],
            send_sem=q_send.at[t],
            recv_sem=q_recv.at[t],
            device_id=(patch_of(z, tx, core), th),
            device_id_type=MESH,
        )

    q_self = pltpu.make_async_copy(
        queries_ref.at[:, pl.ds(pl.multiple_of(head * width, LANES), width)],
        qbuf.at[pl.ds(pl.multiple_of(head * small, small), small), :],
        q_recv.at[0],
    )
    q_self.start()

    @pl.loop(1, 2 * nh)
    def _(t):
        q_copy(t).start()

    def ring_copy(j, s, way):
        slot = lax.rem(z + nz - s, nz) if way == 0 else lax.rem(z + s, nz)
        ref = codes.at[j, slot]
        if s == nz // 2 - 1:
            ref = ref.at[pl.ds(way * half, half)]
        return pltpu.make_async_remote_copy(
            src_ref=ref,
            dst_ref=ref,
            send_sem=ring_send.at[j, s, way],
            recv_sem=ring_recv.at[j, s, way],
            device_id=right if way == 0 else left,
            device_id_type=MESH,
        )

    def old_rows(j, side, patch_id):
        return stale[2 * j + side][owner_ref[patch_id]].astype(F32)

    def encode(j):
        lanes = slice(j * LANES, (j + 1) * LANES)
        delta = jnp.concatenate(
            [fresh[i, :, lanes].astype(F32) - old_rows(j, i, patch) for i in range(2)], axis=1
        )
        first = delta.astype(BF16)
        rest = delta - first.astype(F32)
        second = rest.astype(BF16)
        third = (rest - second.astype(F32)).astype(BF16)
        total = across(third, basis[j])
        total += across(second, basis[j])
        total += across(first, basis[j])
        codes[j, z] = total.astype(BF16)
        for way in range(2):
            ring_copy(j, 0, way).start()

    def decode(j, slot, chunk, side):
        patch_id = patch_of(slot, xh, core)
        count = step_ref[patch_id].astype(F32)
        pairs = count * (count - 1.0)
        keep = 0.5 - 0.25 * count + 0.0625 * pairs - (pairs * (count - 2.0)) * (1 / 6) * 0.0625
        blend = 1.0 - keep
        grown = jnp.dot(codes[j, slot], basis[j], preferred_element_type=F32)
        new_k = (old_rows(j, 0, patch_id) + blend * grown[:, :LANES]).astype(BF16)
        new_v = (old_rows(j, 1, patch_id) + blend * grown[:, LANES:]).astype(BF16)
        at = slice(side * rows, (side + 1) * rows)
        keys[j, chunk, at] = new_k
        values[j, chunk, at, :LANES] = new_v
        if chunk == 0 and side == 1:
            own_keys[j, at] = new_k
            own_values[j, at, :LANES] = new_v

    def arrive(j, s):
        for way in range(2):
            ring_copy(j, s, way).wait_recv()
        if s < nz // 2 - 1:
            for way in range(2):
                ring_copy(j, s + 1, way).start()
            decode(j, lax.rem(z + nz - 1 - s, nz), s, 1)
            decode(j, lax.rem(z + 1 + s, nz), s + 1, 0)
        else:
            decode(j, lax.rem(z + nz // 2, nz), s, 1)

    def part(j, at, k, v, first):
        q = qbuf[at, j * LANES : (j + 1) * LANES]
        scores = across(q, k)
        top = jnp.max(scores, axis=1, keepdims=True)
        if first:
            now = jnp.broadcast_to(top, (q.shape[0], LANES))
        else:
            before = best[j, at]
            now = jnp.maximum(before, top)
        weights = jnp.exp2(scores * scale - now[:, :1] * scale).astype(BF16)
        added = jnp.dot(weights, v, preferred_element_type=F32)
        if first:
            acc[j, at] = added
        else:
            factor = jnp.exp2((before - now) * scale)
            acc[j, at, :LANES] = acc[j, at, :LANES] * factor + added[:, :LANES]
            acc[j, at, LANES:] = acc[j, at, LANES:] * factor + added[:, LANES:]
        best[j, at] = now

    def attend(j, chunk):
        if chunk == 0:
            part(j, slice(0, rows), own_keys[j], own_values[j], True)
            part(j, slice(rows, 4 * rows), keys[j, 0], values[j, 0], True)
        else:
            part(j, slice(0, 4 * rows), keys[j, chunk], values[j, chunk], False)

    row_id = lax.broadcasted_iota(jnp.int32, (LANES, LANES), 0)
    lane_id = lax.broadcasted_iota(jnp.int32, (LANES, LANES), 1)
    diagonal = row_id == lane_id

    def pack(column):
        return jnp.sum(jnp.where(diagonal, column, 0.0), axis=0, keepdims=True)

    def unpack(line):
        return jnp.sum(
            jnp.where(diagonal, jnp.broadcast_to(line, (LANES, LANES)), 0.0),
            axis=1,
            keepdims=True,
        )

    def local_result(j, at):
        total = acc[j, at, LANES:]
        level = best[j, at] * scale + jnp.log(total) * LOG2E
        return acc[j, at, :LANES] / total, level

    def part_copy(j, which):
        src, dst = ((part_out, got_out), (part_stat, got_stat))[which]
        return pltpu.make_async_remote_copy(
            src_ref=src.at[j],
            dst_ref=dst.at[j],
            send_sem=part_send.at[j, which],
            recv_sem=part_recv.at[j, which],
            device_id=partner,
            device_id_type=MESH,
        )

    def share(j):
        lines = []
        for g in range(2 * groups):
            result, level = local_result(j, pl.ds(2 * rows + g * LANES, LANES))
            part_out[j, g * LANES : (g + 1) * LANES] = result.astype(BF16)
            lines.append(pack(level))
        pad = part_stat.shape[1] - len(lines)
        if pad:
            lines.append(jnp.zeros((pad, LANES), F32))
        part_stat[j] = jnp.concatenate(lines, axis=0)
        for which in range(2):
            part_copy(j, which).start()

    def mix(result_a, level_a, result_b, level_b):
        share_a = 1.0 / (1.0 + jnp.exp2(level_b - level_a))
        return result_a * share_a + result_b * (1.0 - share_a)

    def merge(j):
        for which in range(2):
            part_copy(j, which).wait_recv()
        for g in range(2 * groups):
            at = slice(g * LANES, (g + 1) * LANES)
            result, level = local_result(j, pl.ds(g * LANES, LANES))
            other = got_out[j, at].astype(F32)
            other_level = unpack(got_stat[j, g : g + 1])
            mixed = mix(result, level, other, other_level)
            sum_out[at, j * LANES : (j + 1) * LANES] = mixed.astype(BF16)
            top = jnp.maximum(level, other_level)
            low = jnp.minimum(level, other_level)
            joint = top + jnp.log(1.0 + jnp.exp2(low - top)) * LOG2E
            sum_stat[g, j : j + 1] = pack(joint)

    def final_refs(t, th):
        src = sum_out.at[
            pl.ds(pl.multiple_of((t // nh) * rows + th * small, small), small), :
        ]
        dst = final_out.at[t // nh, :, pl.ds(pl.multiple_of(head * width, LANES), width)]
        stat_src = sum_stat.at[(t // nh) * groups + th // per_group]
        stat_dst = final_stat.at[t // nh, head]
        return (src, dst), (stat_src, stat_dst)

    def final_copy(t, which):
        tx, th = plane(t)
        src, dst = final_refs(t, th)[which]
        return pltpu.make_async_remote_copy(
            src_ref=src,
            dst_ref=dst,
            send_sem=final_send.at[which, t],
            recv_sem=final_recv.at[which, t],
            device_id=(patch_of(z, tx, core), th),
            device_id_type=MESH,
        )

    for load in loads[:2]:
        load.wait()
    for j in range(heads):
        loads[2 + 2 * j].wait()
        loads[3 + 2 * j].wait()
        encode(j)

    q_self.wait()

    @pl.loop(1, 2 * nh)
    def _(t):
        q_copy(t).wait_recv()

    q_cross = pltpu.make_async_remote_copy(
        src_ref=qbuf.at[pl.ds(0, 2 * rows)],
        dst_ref=qbuf.at[pl.ds(2 * rows, 2 * rows)],
        send_sem=qc_sem.at[0],
        recv_sem=qc_sem.at[1],
        device_id=partner,
        device_id_type=MESH,
    )
    q_cross.start()

    for j in range(heads):
        own_keys[j, :rows] = fresh[0, :, j * LANES : (j + 1) * LANES]
        own_values[j, :rows, :LANES] = fresh[1, :, j * LANES : (j + 1) * LANES]
        decode(j, z, 0, 0)
    for j in range(heads):
        arrive(j, 0)
    q_cross.wait_recv()

    steps = nz // 2
    items = [(s, j) for s in range(steps) for j in range(heads)]
    seen = heads
    for i, (s, j) in enumerate(items):
        ahead = 2 if s == 0 else 1
        while seen <= i or (seen < i + ahead and seen < 2 * heads):
            arrive(items[seen][1], items[seen][0])
            seen += 1
        attend(j, s)
        if s == steps - 1:
            share(j)

    for j in range(heads):
        merge(j)

    (src, dst), (stat_src, stat_dst) = final_refs(0, head)
    final_self = [
        pltpu.make_async_copy(src, dst, final_recv.at[0, 0]),
        pltpu.make_async_copy(stat_src, stat_dst, final_recv.at[1, 0]),
    ]
    for copy in final_self:
        copy.start()

    @pl.loop(1, 2 * nh)
    def _(t):
        for which in range(2):
            final_copy(t, which).start()

    for copy in final_self:
        copy.wait()

    @pl.loop(1, 2 * nh)
    def _(t):
        for which in range(2):
            final_copy(t, which).wait_recv()

    lane = lax.broadcasted_iota(jnp.int32, (small, LANES), 1)
    row = lax.broadcasted_iota(jnp.int32, (small, LANES), 0)
    mine = lane == row + lax.rem(head, per_group) * small

    def pick(line):
        return jnp.sum(
            jnp.where(mine, jnp.broadcast_to(line, (small, LANES)), 0.0), axis=1, keepdims=True
        )

    @pl.loop(0, nh)
    def _(g):
        for j in range(heads):
            lanes = pl.ds(pl.multiple_of((g * heads + j) * LANES, LANES), LANES)
            results = [final_out[x, :, lanes].astype(F32) for x in range(2)]
            levels = [pick(final_stat[x, g, j : j + 1]) for x in range(2)]
            mixed = mix(results[0], levels[0], results[1], levels[1])
            out_ref[:, lanes] = mixed.astype(BF16)

    @pl.loop(1, 2 * nh)
    def _(t):
        q_copy(t).wait_send()
        for which in range(2):
            final_copy(t, which).wait_send()

    q_cross.wait_send()
    for j in range(heads):
        for s in range(steps):
            for way in range(2):
                ring_copy(j, s, way).wait_send()
        for which in range(2):
            part_copy(j, which).wait_send()


def make_local(nz, nh):
    def local(
        queries,
        fresh_keys,
        fresh_values,
        stale_keys,
        stale_values,
        key_basis,
        value_basis,
        owner_table,
        step_counter,
    ):
        heads = key_basis.shape[0]
        rows = fresh_keys.shape[0]
        small = queries.shape[0]
        width = heads * LANES
        seq = stale_keys.shape[0]
        chunks = nz // 2
        groups = rows // LANES
        smem = pl.BlockSpec(memory_space=pltpu.SMEM)
        hbm = pl.BlockSpec(memory_space=pl.ANY)
        vmem = pl.BlockSpec(memory_space=pltpu.VMEM)
        dma = pltpu.SemaphoreType.DMA
        scratch = [
            [pltpu.VMEM((seq // rows, rows, LANES), BF16) for _ in range(2 * heads)],
            pltpu.VMEM((2, rows, width), BF16),
            pltpu.VMEM((heads, LANES, 2 * LANES), BF16),
            pltpu.VMEM((4 * rows, width), BF16),
            pltpu.VMEM((heads, nz, rows, LANES), BF16),
            pltpu.VMEM((heads, chunks, 2 * rows, LANES), BF16),
            pltpu.VMEM((heads, chunks, 2 * rows, 2 * LANES), BF16),
            pltpu.VMEM((heads, 2 * rows, LANES), BF16),
            pltpu.VMEM((heads, 2 * rows, 2 * LANES), BF16),
            pltpu.VMEM((heads, 4 * rows, 2 * LANES), F32),
            pltpu.VMEM((heads, 4 * rows, LANES), F32),
            pltpu.VMEM((heads, 2 * rows, LANES), BF16),
            pltpu.VMEM((heads, 8, LANES), F32),
            pltpu.VMEM((heads, 2 * rows, LANES), BF16),
            pltpu.VMEM((heads, 8, LANES), F32),
            pltpu.VMEM((2 * rows, width), BF16),
            pltpu.VMEM((2 * groups, 8, LANES), F32),
            pltpu.VMEM((2, small, nh * width), BF16),
            pltpu.VMEM((2, nh, 8, LANES), F32),
            dma((2 + 2 * heads,)),
            dma((2 * nh,)),
            dma((2 * nh,)),
            dma((2,)),
            dma((heads, chunks, 2)),
            dma((heads, chunks, 2)),
            dma((heads, 2)),
            dma((heads, 2)),
            dma((2, 2 * nh)),
            dma((2, 2 * nh)),
        ]
        return pl.pallas_call(
            functools.partial(kernel, (heads, nz, nh, rows)),
            out_shape=jax.ShapeDtypeStruct((small, nh * width), BF16),
            in_specs=[smem, smem, hbm, hbm, hbm, hbm, hbm, vmem, vmem],
            out_specs=vmem,
            scratch_shapes=scratch,
            compiler_params=pltpu.CompilerParams(
                collective_id=0, has_side_effects=True, vmem_limit_bytes=48 << 20
            ),
            name="patch_attention",
        )(
            owner_table,
            step_counter,
            queries,
            fresh_keys,
            fresh_values,
            stale_keys.reshape(seq // rows, rows, width),
            stale_values.reshape(seq // rows, rows, width),
            jnp.swapaxes(key_basis, 1, 2),
            jnp.swapaxes(value_basis, 1, 2),
        )

    return local


def solution(mesh):
    in_specs = (
        P(("patch", "head"), None),
        P("patch", "head"),
        P("patch", "head"),
        P(None, "head"),
        P(None, "head"),
        P("head", None, None),
        P("head", None, None),
        P(),
        P(),
    )
    out_specs = P(("patch", "head"), None)
    local = make_local(mesh.shape["patch"] // 4, mesh.shape["head"])
    return jax.shard_map(local, mesh=mesh, in_specs=in_specs, out_specs=out_specs, check_vma=False)
```

```python
import functools
import math

import jax
import jax.numpy as jnp
from jax import lax
from jax.experimental import pallas as pl
from jax.experimental.pallas import tpu as pltpu
from jax.sharding import PartitionSpec as P

MESH = pl.DeviceIdType.MESH
F32 = jnp.float32
BF16 = jnp.bfloat16
LOG2E = math.log2(math.e)
LANES = 128


def across(a, b):
    return lax.dot_general(a, b, (((1,), (1,)), ((), ())), preferred_element_type=F32)


def kernel(
    dims,
    owner_ref,
    step_ref,
    queries_ref,
    fresh_k_ref,
    fresh_v_ref,
    stale_k_ref,
    stale_v_ref,
    basis_k_ref,
    basis_v_ref,
    out_ref,
    owner_smem,
    step_smem,
    basis_in,
    stale,
    fresh,
    basis,
    qbuf,
    codes,
    keys,
    values,
    own_keys,
    own_values,
    acc,
    best,
    part_out,
    part_stat,
    got_out,
    got_stat,
    sum_out,
    sum_stat,
    final_out,
    final_stat,
    load_sem,
    q_send,
    q_recv,
    qc_sem,
    ring_send,
    ring_recv,
    part_send,
    part_recv,
    final_send,
    final_recv,
):
    heads, nz, nh, rows = dims
    width = heads * LANES
    small = rows // nh
    per_group = LANES // small
    groups = rows // LANES
    scale = LOG2E / math.sqrt(LANES)

    patch = lax.axis_index("patch")
    head = lax.axis_index("head")
    core = lax.rem(patch, 2)
    xh = lax.rem(patch // 2, 2)
    z = patch // 4

    def patch_of(z_, x_, c_):
        return (z_ * 2 + x_) * 2 + c_

    partner = (patch_of(z, xh, 1 - core), head)
    right = (patch_of(lax.rem(z + 1, nz), xh, core), head)
    left = (patch_of(lax.rem(z + nz - 1, nz), xh, core), head)

    def plane(t):
        tx = lax.rem(xh + t // nh, 2)
        th = lax.rem(head + lax.rem(t, nh), nh)
        return tx, th

    loads = []
    for i, src in enumerate((fresh_k_ref, fresh_v_ref)):
        loads.append(pltpu.make_async_copy(src, fresh.at[i], load_sem.at[i]))
    for j in range(heads):
        for i, src in enumerate((stale_k_ref, stale_v_ref)):
            loads.append(
                pltpu.make_async_copy(
                    src.at[:, :, j * LANES : (j + 1) * LANES],
                    stale[2 * j + i],
                    load_sem.at[2 + 2 * j + i],
                )
            )
    small_loads = [
        pltpu.make_async_copy(src, dst, load_sem.at[2 + 2 * heads + i])
        for i, (src, dst) in enumerate(
            (
                (owner_ref, owner_smem),
                (step_ref, step_smem),
                (basis_k_ref, basis_in.at[0]),
                (basis_v_ref, basis_in.at[1]),
            )
        )
    ]
    for load in small_loads + loads:
        load.start()

    barrier = pltpu.get_barrier_semaphore()
    for device in (partner, right, left):
        pl.semaphore_signal(barrier, inc=1, device_id=device, device_id_type=MESH)

    @pl.loop(1, 2 * nh)
    def _(t):
        tx, th = plane(t)
        pl.semaphore_signal(
            barrier, inc=1, device_id=(patch_of(z, tx, core), th), device_id_type=MESH
        )

    for load in small_loads:
        load.wait()
    rank = basis_k_ref.shape[1]
    blank = jnp.zeros((rank, LANES), BF16)
    for j in range(heads):
        basis[j, :rank, :LANES] = basis_in[0, j]
        basis[j, :rank, LANES:] = blank
        basis[j, rank:, :LANES] = blank
        basis[j, rank:, LANES:] = basis_in[1, j]
    pl.semaphore_wait(barrier, 3 + 2 * nh - 1)

    def q_lanes(th, j):
        return pl.ds(pl.multiple_of(th * width + j * LANES, LANES), LANES)

    def q_copy(t, j):
        tx, th = plane(t)
        start = pl.multiple_of((t // nh) * rows + head * small, small)
        return pltpu.make_async_remote_copy(
            src_ref=queries_ref.at[:, q_lanes(th, j)],
            dst_ref=qbuf.at[j, pl.ds(start, small)],
            send_sem=q_send.at[j, t],
            recv_sem=q_recv.at[j, t],
            device_id=(patch_of(z, tx, core), th),
            device_id_type=MESH,
        )

    def q_self(j):
        return pltpu.make_async_copy(
            queries_ref.at[:, q_lanes(head, j)],
            qbuf.at[j, pl.ds(pl.multiple_of(head * small, small), small)],
            q_recv.at[j, 0],
        )

    def q_start(j):
        q_self(j).start()

        @pl.loop(1, 2 * nh)
        def _(t):
            q_copy(t, j).start()

    def q_cross(j):
        return pltpu.make_async_remote_copy(
            src_ref=qbuf.at[j, pl.ds(0, 2 * rows)],
            dst_ref=qbuf.at[j, pl.ds(2 * rows, 2 * rows)],
            send_sem=qc_sem.at[0, j],
            recv_sem=qc_sem.at[1, j],
            device_id=partner,
            device_id_type=MESH,
        )

    def q_arrive(j):
        q_self(j).wait()

        @pl.loop(1, 2 * nh)
        def _(t):
            q_copy(t, j).wait_recv()

        q_cross(j).start()

    mid = nz // 2
    slow = z // mid
    fast = 1 - slow
    to_end = z + slow * (nz - 1 - 2 * z)

    def source(s, way):
        return lax.rem(z + 2 * nz - (1 - 2 * way) * s, nz)

    def ring_copy(j, s, way):
        ref = codes.at[j, source(s, way)]
        return pltpu.make_async_remote_copy(
            src_ref=ref,
            dst_ref=ref,
            send_sem=ring_send.at[j, s, way],
            recv_sem=ring_recv.at[j, s, way],
            device_id=(patch_of(lax.rem(z + nz + 1 - 2 * way, nz), xh, core), head),
            device_id_type=MESH,
        )

    def last_hop(way):
        if way is fast:
            return z * (nz - 1 - z) > 0
        return (z - mid) * (z - mid + 1) == 0

    def pass_on(j, s, way):
        ring_copy(j, s, way).wait_recv()
        if s < mid - 2:
            ring_copy(j, s + 1, way).start()
        elif s == mid - 2:

            @pl.when(last_hop(way))
            def _():
                ring_copy(j, s + 1, way).start()

    def old_rows(j, side, patch_id):
        return stale[2 * j + side][owner_smem[patch_id]].astype(F32)

    def encode(j):
        lanes = slice(j * LANES, (j + 1) * LANES)
        delta = jnp.concatenate(
            [fresh[i, :, lanes].astype(F32) - old_rows(j, i, patch) for i in range(2)], axis=1
        )
        first = delta.astype(BF16)
        rest = delta - first.astype(F32)
        second = rest.astype(BF16)
        third = (rest - second.astype(F32)).astype(BF16)
        total = across(third, basis[j])
        total += across(second, basis[j])
        total += across(first, basis[j])
        codes[j, z] = total.astype(BF16)
        for way in range(2):
            ring_copy(j, 0, way).start()

    def decode(j, slot, chunk, side):
        patch_id = patch_of(slot, xh, core)
        count = step_smem[patch_id].astype(F32)
        pairs = count * (count - 1.0)
        keep = 0.5 - 0.25 * count + 0.0625 * pairs - (pairs * (count - 2.0)) * (1 / 6) * 0.0625
        blend = 1.0 - keep
        grown = jnp.dot(codes[j, slot], basis[j], preferred_element_type=F32)
        new_k = (old_rows(j, 0, patch_id) + blend * grown[:, :LANES]).astype(BF16)
        new_v = (old_rows(j, 1, patch_id) + blend * grown[:, LANES:]).astype(BF16)
        at = slice(side * rows, (side + 1) * rows)
        keys[j, chunk, at] = new_k
        values[j, chunk, at, :LANES] = new_v
        if chunk == 0 and side == 1:
            own_keys[j, at] = new_k
            own_values[j, at, :LANES] = new_v

    def arrive(j, s):
        pass_on(j, s, fast)
        if s < mid - 1:

            @pl.when(to_end > s)
            def _():
                pass_on(j, s, slow)

        decode(j, source(s + 1, fast), s, 1 if s == 0 else 0)
        if s > 0:

            @pl.when(to_end <= s - 1)
            def _():
                pass_on(j, s - 1, slow)

            decode(j, source(s, slow), s, 1)

    def part(j, at, k, v, first):
        q = qbuf[j, at]
        scores = across(q, k)
        top = jnp.max(scores, axis=1, keepdims=True)
        if first:
            now = jnp.broadcast_to(top, (q.shape[0], LANES))
        else:
            before = best[j, at]
            now = jnp.maximum(before, top)
        weights = jnp.exp2(scores * scale - now[:, :1] * scale).astype(BF16)
        added = jnp.dot(weights, v, preferred_element_type=F32)
        if first:
            acc[j, at] = added
        else:
            factor = jnp.exp2((before - now) * scale)
            acc[j, at, :LANES] = acc[j, at, :LANES] * factor + added[:, :LANES]
            acc[j, at, LANES:] = acc[j, at, LANES:] * factor + added[:, LANES:]
        best[j, at] = now

    def attend(j, chunk):
        if chunk == 0:
            part(j, slice(0, rows), own_keys[j], own_values[j], True)
            part(j, slice(rows, 4 * rows), keys[j, 0], values[j, 0], True)
        else:
            part(j, slice(0, 4 * rows), keys[j, chunk], values[j, chunk], False)

    row_id = lax.broadcasted_iota(jnp.int32, (LANES, LANES), 0)
    lane_id = lax.broadcasted_iota(jnp.int32, (LANES, LANES), 1)
    diagonal = row_id == lane_id

    def pack(column):
        return jnp.sum(jnp.where(diagonal, column, 0.0), axis=0, keepdims=True)

    def unpack(line):
        return jnp.sum(
            jnp.where(diagonal, jnp.broadcast_to(line, (LANES, LANES)), 0.0),
            axis=1,
            keepdims=True,
        )

    def local_result(j, at):
        total = acc[j, at, LANES:]
        level = best[j, at] * scale + jnp.log(total) * LOG2E
        return acc[j, at, :LANES] / total, level

    def part_copy(j, which):
        src, dst = ((part_out, got_out), (part_stat, got_stat))[which]
        return pltpu.make_async_remote_copy(
            src_ref=src.at[j],
            dst_ref=dst.at[j],
            send_sem=part_send.at[j, which],
            recv_sem=part_recv.at[j, which],
            device_id=partner,
            device_id_type=MESH,
        )

    def share(j):
        lines = []
        for g in range(2 * groups):
            result, level = local_result(j, pl.ds(2 * rows + g * LANES, LANES))
            part_out[j, g * LANES : (g + 1) * LANES] = result.astype(BF16)
            lines.append(pack(level))
        pad = part_stat.shape[1] - len(lines)
        if pad:
            lines.append(jnp.zeros((pad, LANES), F32))
        part_stat[j] = jnp.concatenate(lines, axis=0)
        for which in range(2):
            part_copy(j, which).start()

    def mix(result_a, level_a, result_b, level_b):
        share_a = 1.0 / (1.0 + jnp.exp2(level_b - level_a))
        return result_a * share_a + result_b * (1.0 - share_a)

    def merge(j):
        for which in range(2):
            part_copy(j, which).wait_recv()
        for g in range(2 * groups):
            at = slice(g * LANES, (g + 1) * LANES)
            result, level = local_result(j, pl.ds(g * LANES, LANES))
            other = got_out[j, at].astype(F32)
            other_level = unpack(got_stat[j, g : g + 1])
            mixed = mix(result, level, other, other_level)
            sum_out[j, at] = mixed.astype(BF16)
            top = jnp.maximum(level, other_level)
            low = jnp.minimum(level, other_level)
            joint = top + jnp.log(1.0 + jnp.exp2(low - top)) * LOG2E
            sum_stat[g, j : j + 1] = pack(joint)

    def final_refs(t, th, j):
        if j == heads:
            src = sum_stat.at[(t // nh) * groups + th // per_group]
            return src, final_stat.at[t // nh, head]
        start = pl.multiple_of((t // nh) * rows + th * small, small)
        return sum_out.at[j, pl.ds(start, small)], final_out.at[t // nh, head, j]

    def final_copy(t, j):
        tx, th = plane(t)
        src, dst = final_refs(t, th, j)
        return pltpu.make_async_remote_copy(
            src_ref=src,
            dst_ref=dst,
            send_sem=final_send.at[j, t],
            recv_sem=final_recv.at[j, t],
            device_id=(patch_of(z, tx, core), th),
            device_id_type=MESH,
        )

    def final_self(j):
        src, dst = final_refs(0, head, j)
        return pltpu.make_async_copy(src, dst, final_recv.at[j, 0])

    def final_start(j):
        final_self(j).start()

        @pl.loop(1, 2 * nh)
        def _(t):
            final_copy(t, j).start()

    for j in range(heads):
        q_start(j)
        if j == 0:
            for load in loads[:2]:
                load.wait()
        loads[2 + 2 * j].wait()
        loads[3 + 2 * j].wait()
        encode(j)

    ones = jnp.ones(values.shape[2:3] + (LANES,), BF16)
    for j in range(heads):
        own_values[j, :, LANES:] = ones
        for chunk in range(nz // 2):
            values[j, chunk, :, LANES:] = ones
        own_keys[j, :rows] = fresh[0, :, j * LANES : (j + 1) * LANES]
        own_values[j, :rows, :LANES] = fresh[1, :, j * LANES : (j + 1) * LANES]
        decode(j, z, 0, 0)
    sum_stat[...] = jnp.zeros(sum_stat.shape, F32)

    for j in range(min(2, heads)):
        q_arrive(j)
        arrive(j, 0)

    steps = nz // 2
    items = [(s, j) for s in range(steps) for j in range(heads)]

    def arrives_after(k):
        if k < 2 * heads:
            return k - heads + (1 if heads > 2 else 0)
        return k - 2 if k <= 3 * heads else k - 1

    for i, (s, j) in enumerate(items):
        if s == 0:
            q_cross(j).wait_recv()
        attend(j, s)
        if s == 0 and j + 2 < heads:
            q_arrive(j + 2)
            arrive(j + 2, 0)
        if s == steps - 1:
            share(j)
            if j == heads - 2:
                for other in range(j):
                    merge(other)
                    final_start(other)
        for k in range(heads, len(items)):
            if arrives_after(k) == i:
                arrive(items[k][1], items[k][0])
    for j in range(max(heads - 2, 0), heads):
        merge(j)
        final_start(j)
    final_start(heads)

    for j in range(heads + 1):
        final_self(j).wait()

    @pl.loop(1, 2 * nh)
    def _(t):
        for j in range(heads + 1):
            final_copy(t, j).wait_recv()

    lane = lax.broadcasted_iota(jnp.int32, (small, LANES), 1)
    row = lax.broadcasted_iota(jnp.int32, (small, LANES), 0)
    mine = lane == row + lax.rem(head, per_group) * small

    def pick(line):
        return jnp.sum(
            jnp.where(mine, jnp.broadcast_to(line, (small, LANES)), 0.0), axis=1, keepdims=True
        )

    @pl.loop(0, nh, unroll=True)
    def _(g):
        for j in range(heads):
            lanes = pl.ds(pl.multiple_of((g * heads + j) * LANES, LANES), LANES)
            results = [final_out[x, g, j].astype(F32) for x in range(2)]
            levels = [pick(final_stat[x, g, j : j + 1]) for x in range(2)]
            mixed = mix(results[0], levels[0], results[1], levels[1])
            out_ref[:, lanes] = mixed.astype(BF16)

    @pl.loop(1, 2 * nh)
    def _(t):
        for j in range(heads):
            q_copy(t, j).wait_send()
        for j in range(heads + 1):
            final_copy(t, j).wait_send()

    for j in range(heads):
        q_cross(j).wait_send()
        for s in range(steps - 1):
            for way in range(2):
                ring_copy(j, s, way).wait_send()
        for way in (fast, slow):

            @pl.when(last_hop(way))
            def _():
                ring_copy(j, steps - 1, way).wait_send()

        for which in range(2):
            part_copy(j, which).wait_send()


def make_local(nz, nh):
    def local(
        queries,
        fresh_keys,
        fresh_values,
        stale_keys,
        stale_values,
        key_basis,
        value_basis,
        owner_table,
        step_counter,
    ):
        heads = key_basis.shape[0]
        rows = fresh_keys.shape[0]
        small = queries.shape[0]
        width = heads * LANES
        seq = stale_keys.shape[0]
        chunks = nz // 2
        groups = rows // LANES
        hbm = pl.BlockSpec(memory_space=pl.ANY)
        vmem = pl.BlockSpec(memory_space=pltpu.VMEM)
        dma = pltpu.SemaphoreType.DMA
        scratch = [
            pltpu.SMEM(owner_table.shape, jnp.int32),
            pltpu.SMEM(step_counter.shape, jnp.int32),
            pltpu.VMEM((2, heads) + key_basis.shape[:0:-1], BF16),
            [pltpu.VMEM((seq // rows, rows, LANES), BF16) for _ in range(2 * heads)],
            pltpu.VMEM((2, rows, width), BF16),
            pltpu.VMEM((heads, LANES, 2 * LANES), BF16),
            pltpu.VMEM((heads, 4 * rows, LANES), BF16),
            pltpu.VMEM((heads, nz, rows, LANES), BF16),
            pltpu.VMEM((heads, chunks, 2 * rows, LANES), BF16),
            pltpu.VMEM((heads, chunks, 2 * rows, 2 * LANES), BF16),
            pltpu.VMEM((heads, 2 * rows, LANES), BF16),
            pltpu.VMEM((heads, 2 * rows, 2 * LANES), BF16),
            pltpu.VMEM((heads, 4 * rows, 2 * LANES), F32),
            pltpu.VMEM((heads, 4 * rows, LANES), F32),
            pltpu.VMEM((heads, 2 * rows, LANES), BF16),
            pltpu.VMEM((heads, 8, LANES), F32),
            pltpu.VMEM((heads, 2 * rows, LANES), BF16),
            pltpu.VMEM((heads, 8, LANES), F32),
            pltpu.VMEM((heads, 2 * rows, LANES), BF16),
            pltpu.VMEM((2 * groups, 8, LANES), F32),
            pltpu.VMEM((2, nh, heads, small, LANES), BF16),
            pltpu.VMEM((2, nh, 8, LANES), F32),
            dma((6 + 2 * heads,)),
            dma((heads, 2 * nh)),
            dma((heads, 2 * nh)),
            dma((2, heads)),
            dma((heads, chunks, 2)),
            dma((heads, chunks, 2)),
            dma((heads, 2)),
            dma((heads, 2)),
            dma((heads + 1, 2 * nh)),
            dma((heads + 1, 2 * nh)),
        ]
        return pl.pallas_call(
            functools.partial(kernel, (heads, nz, nh, rows)),
            out_shape=jax.ShapeDtypeStruct((small, nh * width), BF16),
            in_specs=[hbm] * 9,
            out_specs=vmem,
            scratch_shapes=scratch,
            compiler_params=pltpu.CompilerParams(
                collective_id=0, has_side_effects=True, vmem_limit_bytes=62 << 20
            ),
            name="patch_attention",
        )(
            owner_table,
            step_counter,
            queries,
            fresh_keys,
            fresh_values,
            stale_keys.reshape(seq // rows, rows, width),
            stale_values.reshape(seq // rows, rows, width),
            jnp.swapaxes(key_basis, 1, 2),
            jnp.swapaxes(value_basis, 1, 2),
        )

    return local


def solution(mesh):
    in_specs = (
        P(("patch", "head"), None),
        P("patch", "head"),
        P("patch", "head"),
        P(None, "head"),
        P(None, "head"),
        P("head", None, None),
        P("head", None, None),
        P(),
        P(),
    )
    out_specs = P(("patch", "head"), None)
    local = make_local(mesh.shape["patch"] // 4, mesh.shape["head"])
    return jax.shard_map(local, mesh=mesh, in_specs=in_specs, out_specs=out_specs, check_vma=False)
```

```python
import functools
import math

import jax
import jax.numpy as jnp
from jax import lax
from jax.experimental import pallas as pl
from jax.experimental.pallas import tpu as pltpu
from jax.sharding import PartitionSpec as P

MESH = pl.DeviceIdType.MESH
F32 = jnp.float32
BF16 = jnp.bfloat16
LOG2E = math.log2(math.e)
LANES = 128


def across(a, b):
    return lax.dot_general(a, b, (((1,), (1,)), ((), ())), preferred_element_type=F32)


def kernel(
    dims,
    owner_ref,
    step_ref,
    queries_ref,
    fresh_k_ref,
    fresh_v_ref,
    stale_k_ref,
    stale_v_ref,
    basis_k_ref,
    basis_v_ref,
    out_ref,
    owner_smem,
    step_smem,
    basis_in,
    stale,
    fresh,
    basis,
    qbuf,
    codes,
    keys,
    values,
    own_keys,
    own_values,
    acc,
    best,
    part_out,
    part_stat,
    got_out,
    got_stat,
    sum_out,
    sum_stat,
    final_out,
    final_stat,
    load_sem,
    q_send,
    q_recv,
    qc_sem,
    ring_send,
    ring_recv,
    part_send,
    part_recv,
    final_send,
    final_recv,
):
    heads, nz, nh, rows = dims
    width = heads * LANES
    small = rows // nh
    per_group = LANES // small
    groups = rows // LANES
    scale = LOG2E / math.sqrt(LANES)

    patch = lax.axis_index("patch")
    head = lax.axis_index("head")
    core = lax.rem(patch, 2)
    xh = lax.rem(patch // 2, 2)
    z = patch // 4

    def patch_of(z_, x_, c_):
        return (z_ * 2 + x_) * 2 + c_

    partner = (patch_of(z, xh, 1 - core), head)
    right = (patch_of(lax.rem(z + 1, nz), xh, core), head)
    left = (patch_of(lax.rem(z + nz - 1, nz), xh, core), head)

    def plane(t):
        tx = lax.rem(xh + t // nh, 2)
        th = lax.rem(head + lax.rem(t, nh), nh)
        return tx, th

    loads = []
    for i, src in enumerate((fresh_k_ref, fresh_v_ref)):
        loads.append(pltpu.make_async_copy(src, fresh.at[i], load_sem.at[i]))
    for j in range(heads):
        for i, src in enumerate((stale_k_ref, stale_v_ref)):
            loads.append(
                pltpu.make_async_copy(
                    src.at[:, :, j * LANES : (j + 1) * LANES],
                    stale[2 * j + i],
                    load_sem.at[2 + 2 * j + i],
                )
            )
    small_loads = [
        pltpu.make_async_copy(src, dst, load_sem.at[2 + 2 * heads + i])
        for i, (src, dst) in enumerate(
            (
                (owner_ref, owner_smem),
                (step_ref, step_smem),
                (basis_k_ref, basis_in.at[0]),
                (basis_v_ref, basis_in.at[1]),
            )
        )
    ]
    for load in small_loads + loads:
        load.start()

    barrier = pltpu.get_barrier_semaphore()
    for device in (partner, right, left):
        pl.semaphore_signal(barrier, inc=1, device_id=device, device_id_type=MESH)

    @pl.loop(1, 2 * nh)
    def _(t):
        tx, th = plane(t)
        pl.semaphore_signal(
            barrier, inc=1, device_id=(patch_of(z, tx, core), th), device_id_type=MESH
        )

    for load in small_loads:
        load.wait()
    rank = basis_k_ref.shape[1]
    blank = jnp.zeros((rank, LANES), BF16)
    for j in range(heads):
        basis[j, :rank, :LANES] = basis_in[0, j]
        basis[j, :rank, LANES:] = blank
        basis[j, rank:, :LANES] = blank
        basis[j, rank:, LANES:] = basis_in[1, j]
    pl.semaphore_wait(barrier, 3 + 2 * nh - 1)

    def q_lanes(th, j):
        return pl.ds(pl.multiple_of(th * width + j * LANES, LANES), LANES)

    def q_copy(t, j):
        tx, th = plane(t)
        start = pl.multiple_of((t // nh) * rows + head * small, small)
        return pltpu.make_async_remote_copy(
            src_ref=queries_ref.at[:, q_lanes(th, j)],
            dst_ref=qbuf.at[j, pl.ds(start, small)],
            send_sem=q_send.at[j, t],
            recv_sem=q_recv.at[j, t],
            device_id=(patch_of(z, tx, core), th),
            device_id_type=MESH,
        )

    def q_self(j):
        return pltpu.make_async_copy(
            queries_ref.at[:, q_lanes(head, j)],
            qbuf.at[j, pl.ds(pl.multiple_of(head * small, small), small)],
            q_recv.at[j, 0],
        )

    def q_start(j):
        q_self(j).start()

        @pl.loop(1, 2 * nh)
        def _(t):
            q_copy(t, j).start()

    def q_cross(j):
        return pltpu.make_async_remote_copy(
            src_ref=qbuf.at[j, pl.ds(0, 2 * rows)],
            dst_ref=qbuf.at[j, pl.ds(2 * rows, 2 * rows)],
            send_sem=qc_sem.at[0, j],
            recv_sem=qc_sem.at[1, j],
            device_id=partner,
            device_id_type=MESH,
        )

    def q_arrive(j):
        q_self(j).wait()

        @pl.loop(1, 2 * nh)
        def _(t):
            q_copy(t, j).wait_recv()

        q_cross(j).start()

    mid = nz // 2
    slow = z // mid
    fast = 1 - slow
    to_end = z + slow * (nz - 1 - 2 * z)

    def source(s, way):
        return lax.rem(z + 2 * nz - (1 - 2 * way) * s, nz)

    def ring_copy(j, s, way):
        ref = codes.at[j, source(s, way)]
        return pltpu.make_async_remote_copy(
            src_ref=ref,
            dst_ref=ref,
            send_sem=ring_send.at[j, s, way],
            recv_sem=ring_recv.at[j, s, way],
            device_id=(patch_of(lax.rem(z + nz + 1 - 2 * way, nz), xh, core), head),
            device_id_type=MESH,
        )

    def last_hop(way):
        if way is fast:
            return z * (nz - 1 - z) > 0
        return (z - mid) * (z - mid + 1) == 0

    def pass_on(j, s, way):
        ring_copy(j, s, way).wait_recv()
        if s < mid - 2:
            ring_copy(j, s + 1, way).start()
        elif s == mid - 2:

            @pl.when(last_hop(way))
            def _():
                ring_copy(j, s + 1, way).start()

    def old_rows(j, side, patch_id):
        return stale[2 * j + side][owner_smem[patch_id]].astype(F32)

    def encode(j):
        lanes = slice(j * LANES, (j + 1) * LANES)
        delta = jnp.concatenate(
            [fresh[i, :, lanes].astype(F32) - old_rows(j, i, patch) for i in range(2)], axis=1
        )
        first = delta.astype(BF16)
        rest = delta - first.astype(F32)
        second = rest.astype(BF16)
        third = (rest - second.astype(F32)).astype(BF16)
        total = across(third, basis[j])
        total += across(second, basis[j])
        total += across(first, basis[j])
        codes[j, z] = total.astype(BF16)
        for way in range(2):
            ring_copy(j, 0, way).start()

    def decode(j, slot, chunk, side):
        patch_id = patch_of(slot, xh, core)
        count = step_smem[patch_id].astype(F32)
        pairs = count * (count - 1.0)
        keep = 0.5 - 0.25 * count + 0.0625 * pairs - (pairs * (count - 2.0)) * (1 / 6) * 0.0625
        blend = 1.0 - keep
        grown = jnp.dot(codes[j, slot], basis[j], preferred_element_type=F32)
        new_k = (old_rows(j, 0, patch_id) + blend * grown[:, :LANES]).astype(BF16)
        new_v = (old_rows(j, 1, patch_id) + blend * grown[:, LANES:]).astype(BF16)
        at = slice(side * rows, (side + 1) * rows)
        keys[j, chunk, at] = new_k
        values[j, chunk, at, :LANES] = new_v
        if chunk == 0 and side == 1:
            own_keys[j, at] = new_k
            own_values[j, at, :LANES] = new_v

    def arrive(j, s):
        pass_on(j, s, fast)
        if s < mid - 1:

            @pl.when(to_end > s)
            def _():
                pass_on(j, s, slow)

        decode(j, source(s + 1, fast), s, 1 if s == 0 else 0)
        if s > 0:

            @pl.when(to_end <= s - 1)
            def _():
                pass_on(j, s - 1, slow)

            decode(j, source(s, slow), s, 1)

    def attend(j, chunk):
        if chunk == 0:
            tiles = (
                (slice(0, rows), own_keys[j], own_values[j]),
                (slice(rows, 5 * rows // 2), keys[j, 0], values[j, 0]),
                (slice(5 * rows // 2, 4 * rows), keys[j, 0], values[j, 0]),
            )
        else:
            tiles = (
                (slice(0, 2 * rows), keys[j, chunk], values[j, chunk]),
                (slice(2 * rows, 4 * rows), keys[j, chunk], values[j, chunk]),
            )

        def score(t):
            at, k, _ = tiles[t]
            return across(qbuf[j, at], k)

        def weigh(t, scores):
            at = tiles[t][0]
            now = jnp.max(scores, axis=1, keepdims=True)
            factor = None
            if chunk == 0:
                now = jnp.broadcast_to(now, (scores.shape[0], LANES))
            else:
                before = best[j, at]
                now = jnp.maximum(before, now)
                factor = jnp.exp2((before - now) * scale)
            best[j, at] = now
            return jnp.exp2(scores * scale - now[:, :1] * scale).astype(BF16), factor

        def add(t, weights, factor):
            at, _, v = tiles[t]
            added = jnp.dot(weights, v, preferred_element_type=F32)
            if chunk == 0:
                acc[j, at] = added
            else:
                acc[j, at, :LANES] = acc[j, at, :LANES] * factor + added[:, :LANES]
                acc[j, at, LANES:] = acc[j, at, LANES:] * factor + added[:, LANES:]

        scores = score(0)
        ready = None
        for t in range(len(tiles)):
            following = score(t + 1) if t + 1 < len(tiles) else None
            weighed = weigh(t, scores)
            if ready is not None:
                add(t - 1, *ready)
            ready, scores = weighed, following
        add(len(tiles) - 1, *ready)

    row_id = lax.broadcasted_iota(jnp.int32, (LANES, LANES), 0)
    lane_id = lax.broadcasted_iota(jnp.int32, (LANES, LANES), 1)
    diagonal = row_id == lane_id

    def pack(column):
        return jnp.sum(jnp.where(diagonal, column, 0.0), axis=0, keepdims=True)

    def unpack(line):
        return jnp.sum(
            jnp.where(diagonal, jnp.broadcast_to(line, (LANES, LANES)), 0.0),
            axis=1,
            keepdims=True,
        )

    def local_result(j, at):
        total = acc[j, at, LANES:]
        level = best[j, at] * scale + jnp.log(total) * LOG2E
        return acc[j, at, :LANES] / total, level

    def part_copy(j, which):
        src, dst = ((part_out, got_out), (part_stat, got_stat))[which]
        return pltpu.make_async_remote_copy(
            src_ref=src.at[j],
            dst_ref=dst.at[j],
            send_sem=part_send.at[j, which],
            recv_sem=part_recv.at[j, which],
            device_id=partner,
            device_id_type=MESH,
        )

    def share(j):
        lines = []
        for g in range(2 * groups):
            result, level = local_result(j, pl.ds(2 * rows + g * LANES, LANES))
            part_out[j, g * LANES : (g + 1) * LANES] = result.astype(BF16)
            lines.append(pack(level))
        pad = part_stat.shape[1] - len(lines)
        if pad:
            lines.append(jnp.zeros((pad, LANES), F32))
        part_stat[j] = jnp.concatenate(lines, axis=0)
        for which in range(2):
            part_copy(j, which).start()

    def share_of(level_a, level_b):
        return 1.0 / (1.0 + jnp.exp2(level_b - level_a))

    def mix(result_a, result_b, share_a):
        return result_a * share_a + result_b * (1.0 - share_a)

    def merge(j):
        for which in range(2):
            part_copy(j, which).wait_recv()
        for g in range(2 * groups):
            at = slice(g * LANES, (g + 1) * LANES)
            result, level = local_result(j, pl.ds(g * LANES, LANES))
            other = got_out[j, at].astype(F32)
            other_level = unpack(got_stat[j, g : g + 1])
            mixed = mix(result, other, share_of(level, other_level))
            sum_out[j, at] = mixed.astype(BF16)
            top = jnp.maximum(level, other_level)
            low = jnp.minimum(level, other_level)
            joint = top + jnp.log(1.0 + jnp.exp2(low - top)) * LOG2E
            sum_stat[g, j : j + 1] = pack(joint)

    def final_refs(t, th, j):
        if j == heads:
            src = sum_stat.at[(t // nh) * groups + th // per_group]
            return src, final_stat.at[t // nh, head]
        start = pl.multiple_of((t // nh) * rows + th * small, small)
        return sum_out.at[j, pl.ds(start, small)], final_out.at[t // nh, head, j]

    def final_copy(t, j):
        tx, th = plane(t)
        src, dst = final_refs(t, th, j)
        return pltpu.make_async_remote_copy(
            src_ref=src,
            dst_ref=dst,
            send_sem=final_send.at[j, t],
            recv_sem=final_recv.at[j, t],
            device_id=(patch_of(z, tx, core), th),
            device_id_type=MESH,
        )

    def final_self(j):
        src, dst = final_refs(0, head, j)
        return pltpu.make_async_copy(src, dst, final_recv.at[j, 0])

    def final_start(j):
        final_self(j).start()

        @pl.loop(1, 2 * nh)
        def _(t):
            final_copy(t, j).start()

    for j in range(heads):
        q_start(j)
        if j == 0:
            for load in loads[:2]:
                load.wait()
        loads[2 + 2 * j].wait()
        loads[3 + 2 * j].wait()
        encode(j)

    ones = jnp.ones(values.shape[2:3] + (LANES,), BF16)
    for j in range(heads):
        own_values[j, :, LANES:] = ones
        for chunk in range(nz // 2):
            values[j, chunk, :, LANES:] = ones
        own_keys[j, :rows] = fresh[0, :, j * LANES : (j + 1) * LANES]
        own_values[j, :rows, :LANES] = fresh[1, :, j * LANES : (j + 1) * LANES]
        decode(j, z, 0, 0)
    sum_stat[...] = jnp.zeros(sum_stat.shape, F32)

    for j in range(heads):
        arrive(j, 0)
        q_arrive(j)

    steps = nz // 2
    items = [(s, j) for s in range(steps) for j in range(heads)]

    def arrives_after(k):
        if k < 3 * heads:
            return k - heads
        return k - 2 if k == 3 * heads else k - 1

    for i, (s, j) in enumerate(items):
        if s == 0:
            q_cross(j).wait_recv()
        attend(j, s)
        if s == steps - 1:
            share(j)
            if j == heads - 2:
                for other in range(j):
                    merge(other)
                    final_start(other)
        for k in range(heads, len(items)):
            if arrives_after(k) == i:
                arrive(items[k][1], items[k][0])
    for j in range(max(heads - 2, 0), heads):
        merge(j)
        final_start(j)
    final_start(heads)

    for j in range(heads + 1):
        final_self(j).wait()

    @pl.loop(1, 2 * nh)
    def _(t):
        for j in range(heads + 1):
            final_copy(t, j).wait_recv()

    lane = lax.broadcasted_iota(jnp.int32, (small, LANES), 1)
    row = lax.broadcasted_iota(jnp.int32, (small, LANES), 0)
    mine = lane == row + lax.rem(head, per_group) * small

    def pick(line):
        return jnp.sum(
            jnp.where(mine, jnp.broadcast_to(line, (small, LANES)), 0.0), axis=1, keepdims=True
        )

    @pl.loop(0, nh, unroll=True)
    def _(g):
        shares = share_of(final_stat[0, g], final_stat[1, g])
        for j in range(heads):
            lanes = pl.ds(pl.multiple_of((g * heads + j) * LANES, LANES), LANES)
            results = [final_out[x, g, j].astype(F32) for x in range(2)]
            mixed = mix(results[0], results[1], pick(shares[j : j + 1]))
            out_ref[:, lanes] = mixed.astype(BF16)

    @pl.loop(1, 2 * nh)
    def _(t):
        for j in range(heads):
            q_copy(t, j).wait_send()
        for j in range(heads + 1):
            final_copy(t, j).wait_send()

    for j in range(heads):
        q_cross(j).wait_send()
        for s in range(steps - 1):
            for way in range(2):
                ring_copy(j, s, way).wait_send()
        for way in (fast, slow):

            @pl.when(last_hop(way))
            def _():
                ring_copy(j, steps - 1, way).wait_send()

        for which in range(2):
            part_copy(j, which).wait_send()


def make_local(nz, nh):
    def local(
        queries,
        fresh_keys,
        fresh_values,
        stale_keys,
        stale_values,
        key_basis,
        value_basis,
        owner_table,
        step_counter,
    ):
        heads = key_basis.shape[0]
        rows = fresh_keys.shape[0]
        small = queries.shape[0]
        width = heads * LANES
        seq = stale_keys.shape[0]
        chunks = nz // 2
        groups = rows // LANES
        hbm = pl.BlockSpec(memory_space=pl.ANY)
        vmem = pl.BlockSpec(memory_space=pltpu.VMEM)
        dma = pltpu.SemaphoreType.DMA
        scratch = [
            pltpu.SMEM(owner_table.shape, jnp.int32),
            pltpu.SMEM(step_counter.shape, jnp.int32),
            pltpu.VMEM((2, heads) + key_basis.shape[:0:-1], BF16),
            [pltpu.VMEM((seq // rows, rows, LANES), BF16) for _ in range(2 * heads)],
            pltpu.VMEM((2, rows, width), BF16),
            pltpu.VMEM((heads, LANES, 2 * LANES), BF16),
            pltpu.VMEM((heads, 4 * rows, LANES), BF16),
            pltpu.VMEM((heads, nz, rows, LANES), BF16),
            pltpu.VMEM((heads, chunks, 2 * rows, LANES), BF16),
            pltpu.VMEM((heads, chunks, 2 * rows, 2 * LANES), BF16),
            pltpu.VMEM((heads, 2 * rows, LANES), BF16),
            pltpu.VMEM((heads, 2 * rows, 2 * LANES), BF16),
            pltpu.VMEM((heads, 4 * rows, 2 * LANES), F32),
            pltpu.VMEM((heads, 4 * rows, LANES), F32),
            pltpu.VMEM((heads, 2 * rows, LANES), BF16),
            pltpu.VMEM((heads, 8, LANES), F32),
            pltpu.VMEM((heads, 2 * rows, LANES), BF16),
            pltpu.VMEM((heads, 8, LANES), F32),
            pltpu.VMEM((heads, 2 * rows, LANES), BF16),
            pltpu.VMEM((2 * groups, 8, LANES), F32),
            pltpu.VMEM((2, nh, heads, small, LANES), BF16),
            pltpu.VMEM((2, nh, 8, LANES), F32),
            dma((6 + 2 * heads,)),
            dma((heads, 2 * nh)),
            dma((heads, 2 * nh)),
            dma((2, heads)),
            dma((heads, chunks, 2)),
            dma((heads, chunks, 2)),
            dma((heads, 2)),
            dma((heads, 2)),
            dma((heads + 1, 2 * nh)),
            dma((heads + 1, 2 * nh)),
        ]
        return pl.pallas_call(
            functools.partial(kernel, (heads, nz, nh, rows)),
            out_shape=jax.ShapeDtypeStruct((small, nh * width), BF16),
            in_specs=[hbm] * 9,
            out_specs=vmem,
            scratch_shapes=scratch,
            compiler_params=pltpu.CompilerParams(
                collective_id=0, has_side_effects=True, vmem_limit_bytes=62 << 20
            ),
            name="patch_attention",
        )(
            owner_table,
            step_counter,
            queries,
            fresh_keys,
            fresh_values,
            stale_keys.reshape(seq // rows, rows, width),
            stale_values.reshape(seq // rows, rows, width),
            jnp.swapaxes(key_basis, 1, 2),
            jnp.swapaxes(value_basis, 1, 2),
        )

    return local


def solution(mesh):
    in_specs = (
        P(("patch", "head"), None),
        P("patch", "head"),
        P("patch", "head"),
        P(None, "head"),
        P(None, "head"),
        P("head", None, None),
        P("head", None, None),
        P(),
        P(),
    )
    out_specs = P(("patch", "head"), None)
    local = make_local(mesh.shape["patch"] // 4, mesh.shape["head"])
    return jax.shard_map(local, mesh=mesh, in_specs=in_specs, out_specs=out_specs, check_vma=False)
```

```python
import functools
import math

import jax
import jax.numpy as jnp
from jax import lax
from jax.experimental import pallas as pl
from jax.experimental.pallas import tpu as pltpu
from jax.sharding import PartitionSpec as P

MESH = pl.DeviceIdType.MESH
F32 = jnp.float32
BF16 = jnp.bfloat16
LOG2E = math.log2(math.e)
LANES = 128


def across(a, b):
    return lax.dot_general(a, b, (((1,), (1,)), ((), ())), preferred_element_type=F32)


def kernel(
    dims,
    owner_ref,
    step_ref,
    queries_ref,
    fresh_k_ref,
    fresh_v_ref,
    stale_k_ref,
    stale_v_ref,
    basis_k_ref,
    basis_v_ref,
    out_ref,
    owner_smem,
    step_smem,
    basis_in,
    stale,
    fresh,
    basis,
    qbuf,
    codes,
    keys,
    values,
    own_keys,
    own_values,
    acc,
    best,
    part_out,
    part_stat,
    got_out,
    got_stat,
    sum_out,
    sum_stat,
    final_out,
    final_stat,
    load_sem,
    q_send,
    q_recv,
    qc_sem,
    ring_send,
    ring_recv,
    part_send,
    part_recv,
    final_send,
    final_recv,
):
    heads, nz, nh, rows = dims
    width = heads * LANES
    small = rows // nh
    per_group = LANES // small
    groups = rows // LANES
    scale = LOG2E / math.sqrt(LANES)

    patch = lax.axis_index("patch")
    head = lax.axis_index("head")
    core = lax.rem(patch, 2)
    xh = lax.rem(patch // 2, 2)
    z = patch // 4

    def patch_of(z_, x_, c_):
        return (z_ * 2 + x_) * 2 + c_

    partner = (patch_of(z, xh, 1 - core), head)
    right = (patch_of(lax.rem(z + 1, nz), xh, core), head)
    left = (patch_of(lax.rem(z + nz - 1, nz), xh, core), head)

    def plane(t):
        tx = lax.rem(xh + t // nh, 2)
        th = lax.rem(head + lax.rem(t, nh), nh)
        return tx, th

    loads = []
    for i, src in enumerate((fresh_k_ref, fresh_v_ref)):
        loads.append(pltpu.make_async_copy(src, fresh.at[i], load_sem.at[i]))
    for j in range(heads):
        for i, src in enumerate((stale_k_ref, stale_v_ref)):
            loads.append(
                pltpu.make_async_copy(
                    src.at[:, :, j * LANES : (j + 1) * LANES],
                    stale[2 * j + i],
                    load_sem.at[2 + 2 * j + i],
                )
            )
    small_loads = [
        pltpu.make_async_copy(src, dst, load_sem.at[2 + 2 * heads + i])
        for i, (src, dst) in enumerate(
            (
                (owner_ref, owner_smem),
                (step_ref, step_smem),
                (basis_k_ref, basis_in.at[0]),
                (basis_v_ref, basis_in.at[1]),
            )
        )
    ]
    for load in small_loads + loads:
        load.start()

    barrier = pltpu.get_barrier_semaphore()
    for device in (partner, right, left):
        pl.semaphore_signal(barrier, inc=1, device_id=device, device_id_type=MESH)

    @pl.loop(1, 2 * nh)
    def _(t):
        tx, th = plane(t)
        pl.semaphore_signal(
            barrier, inc=1, device_id=(patch_of(z, tx, core), th), device_id_type=MESH
        )

    for load in small_loads:
        load.wait()
    rank = basis_k_ref.shape[1]
    blank = jnp.zeros((rank, LANES), BF16)
    for j in range(heads):
        basis[j, :rank, :LANES] = basis_in[0, j]
        basis[j, :rank, LANES:] = blank
        basis[j, rank:, :LANES] = blank
        basis[j, rank:, LANES:] = basis_in[1, j]
    pl.semaphore_wait(barrier, 3 + 2 * nh - 1)

    def q_lanes(th, j):
        return pl.ds(pl.multiple_of(th * width + j * LANES, LANES), LANES)

    def q_copy(t, j):
        tx, th = plane(t)
        start = pl.multiple_of((t // nh) * rows + head * small, small)
        return pltpu.make_async_remote_copy(
            src_ref=queries_ref.at[:, q_lanes(th, j)],
            dst_ref=qbuf.at[j, pl.ds(start, small)],
            send_sem=q_send.at[j, t],
            recv_sem=q_recv.at[j, t],
            device_id=(patch_of(z, tx, core), th),
            device_id_type=MESH,
        )

    def q_self(j):
        return pltpu.make_async_copy(
            queries_ref.at[:, q_lanes(head, j)],
            qbuf.at[j, pl.ds(pl.multiple_of(head * small, small), small)],
            q_recv.at[j, 0],
        )

    def q_start(j):
        q_self(j).start()

        @pl.loop(1, 2 * nh)
        def _(t):
            q_copy(t, j).start()

    def q_cross(j):
        return pltpu.make_async_remote_copy(
            src_ref=qbuf.at[j, pl.ds(0, 2 * rows)],
            dst_ref=qbuf.at[j, pl.ds(2 * rows, 2 * rows)],
            send_sem=qc_sem.at[0, j],
            recv_sem=qc_sem.at[1, j],
            device_id=partner,
            device_id_type=MESH,
        )

    def q_arrive(j):
        q_self(j).wait()

        @pl.loop(1, 2 * nh)
        def _(t):
            q_copy(t, j).wait_recv()

        q_cross(j).start()

    mid = nz // 2
    slow = z // mid
    fast = 1 - slow
    to_end = z + slow * (nz - 1 - 2 * z)

    def source(s, way):
        return lax.rem(z + 2 * nz - (1 - 2 * way) * s, nz)

    def ring_copy(j, s, way):
        ref = codes.at[j, source(s, way)]
        return pltpu.make_async_remote_copy(
            src_ref=ref,
            dst_ref=ref,
            send_sem=ring_send.at[j, s, way],
            recv_sem=ring_recv.at[j, s, way],
            device_id=(patch_of(lax.rem(z + nz + 1 - 2 * way, nz), xh, core), head),
            device_id_type=MESH,
        )

    def last_hop(way):
        if way is fast:
            return z * (nz - 1 - z) > 0
        return (z - mid) * (z - mid + 1) == 0

    def pass_on(j, s, way):
        ring_copy(j, s, way).wait_recv()
        if s < mid - 2:
            ring_copy(j, s + 1, way).start()
        elif s == mid - 2:

            @pl.when(last_hop(way))
            def _():
                ring_copy(j, s + 1, way).start()

    def old_rows(j, side, patch_id):
        return stale[2 * j + side][owner_smem[patch_id]].astype(F32)

    def encode(j):
        lanes = slice(j * LANES, (j + 1) * LANES)
        delta = jnp.concatenate(
            [fresh[i, :, lanes].astype(F32) - old_rows(j, i, patch) for i in range(2)], axis=1
        )
        first = delta.astype(BF16)
        rest = delta - first.astype(F32)
        second = rest.astype(BF16)
        third = (rest - second.astype(F32)).astype(BF16)
        total = across(third, basis[j])
        total += across(second, basis[j])
        total += across(first, basis[j])
        codes[j, z] = total.astype(BF16)
        for way in range(2):
            ring_copy(j, 0, way).start()

    def decode(j, slot, chunk, side):
        patch_id = patch_of(slot, xh, core)
        count = step_smem[patch_id].astype(F32)
        pairs = count * (count - 1.0)
        keep = 0.5 - 0.25 * count + 0.0625 * pairs - (pairs * (count - 2.0)) * (1 / 6) * 0.0625
        blend = 1.0 - keep
        grown = jnp.dot(codes[j, slot], basis[j], preferred_element_type=F32)
        new_k = (old_rows(j, 0, patch_id) + blend * grown[:, :LANES]).astype(BF16)
        new_v = (old_rows(j, 1, patch_id) + blend * grown[:, LANES:]).astype(BF16)
        at = slice(side * rows, (side + 1) * rows)
        keys[j, chunk, at] = new_k
        values[j, chunk, at, :LANES] = new_v
        if chunk == 0 and side == 1:
            own_keys[j, at] = new_k
            own_values[j, at, :LANES] = new_v

    def arrive(j, s):
        pass_on(j, s, fast)
        if s < mid - 1:

            @pl.when(to_end > s)
            def _():
                pass_on(j, s, slow)

        if s > 0:

            @pl.when(to_end <= s - 1)
            def _():
                pass_on(j, s - 1, slow)

        decode(j, source(s + 1, fast), s, 1 if s == 0 else 0)
        if s > 0:
            decode(j, source(s, slow), s, 1)

    def attend(j, chunk):
        if chunk == 0:
            tiles = (
                (slice(0, rows), own_keys[j], own_values[j]),
                (slice(rows, 5 * rows // 2), keys[j, 0], values[j, 0]),
                (slice(5 * rows // 2, 4 * rows), keys[j, 0], values[j, 0]),
            )
        else:
            tiles = (
                (slice(0, 2 * rows), keys[j, chunk], values[j, chunk]),
                (slice(2 * rows, 4 * rows), keys[j, chunk], values[j, chunk]),
            )

        def score(t):
            at, k, _ = tiles[t]
            return across(qbuf[j, at], k)

        def weigh(t, scores):
            at = tiles[t][0]
            now = jnp.max(scores, axis=1, keepdims=True)
            factor = None
            if chunk == 0:
                now = jnp.broadcast_to(now, (scores.shape[0], LANES))
            else:
                before = best[j, at]
                now = jnp.maximum(before, now)
                factor = jnp.exp2((before - now) * scale)
            best[j, at] = now
            return jnp.exp2(scores * scale - now[:, :1] * scale).astype(BF16), factor

        def add(t, weights, factor):
            at, _, v = tiles[t]
            added = jnp.dot(weights, v, preferred_element_type=F32)
            if chunk == 0:
                acc[j, at] = added
            else:
                acc[j, at, :LANES] = acc[j, at, :LANES] * factor + added[:, :LANES]
                acc[j, at, LANES:] = acc[j, at, LANES:] * factor + added[:, LANES:]

        scores = score(0)
        ready = None
        for t in range(len(tiles)):
            following = score(t + 1) if t + 1 < len(tiles) else None
            weighed = weigh(t, scores)
            if ready is not None:
                add(t - 1, *ready)
            ready, scores = weighed, following
        add(len(tiles) - 1, *ready)

    row_id = lax.broadcasted_iota(jnp.int32, (LANES, LANES), 0)
    lane_id = lax.broadcasted_iota(jnp.int32, (LANES, LANES), 1)
    diagonal = row_id == lane_id

    def pack(column):
        return jnp.sum(jnp.where(diagonal, column, 0.0), axis=0, keepdims=True)

    def unpack(line):
        return jnp.sum(
            jnp.where(diagonal, jnp.broadcast_to(line, (LANES, LANES)), 0.0),
            axis=1,
            keepdims=True,
        )

    def local_result(j, at):
        total = acc[j, at, LANES:]
        level = best[j, at] * scale + jnp.log(total) * LOG2E
        return acc[j, at, :LANES] / total, level

    def part_copy(j, which):
        src, dst = ((part_out, got_out), (part_stat, got_stat))[which]
        return pltpu.make_async_remote_copy(
            src_ref=src.at[j],
            dst_ref=dst.at[j],
            send_sem=part_send.at[j, which],
            recv_sem=part_recv.at[j, which],
            device_id=partner,
            device_id_type=MESH,
        )

    def share(j):
        lines = []
        for g in range(2 * groups):
            result, level = local_result(j, pl.ds(2 * rows + g * LANES, LANES))
            part_out[j, g * LANES : (g + 1) * LANES] = result.astype(BF16)
            lines.append(pack(level))
        pad = part_stat.shape[1] - len(lines)
        if pad:
            lines.append(jnp.zeros((pad, LANES), F32))
        part_stat[j] = jnp.concatenate(lines, axis=0)
        for which in range(2):
            part_copy(j, which).start()

    def share_of(level_a, level_b):
        return 1.0 / (1.0 + jnp.exp2(level_b - level_a))

    def mix(result_a, result_b, share_a):
        return result_a * share_a + result_b * (1.0 - share_a)

    def merge(j):
        for which in range(2):
            part_copy(j, which).wait_recv()
        for g in range(2 * groups):
            at = slice(g * LANES, (g + 1) * LANES)
            result, level = local_result(j, pl.ds(g * LANES, LANES))
            other = got_out[j, at].astype(F32)
            other_level = unpack(got_stat[j, g : g + 1])
            mixed = mix(result, other, share_of(level, other_level))
            sum_out[j, at] = mixed.astype(BF16)
            top = jnp.maximum(level, other_level)
            low = jnp.minimum(level, other_level)
            joint = top + jnp.log(1.0 + jnp.exp2(low - top)) * LOG2E
            sum_stat[g, j : j + 1] = pack(joint)

    def final_refs(t, th, j):
        if j == heads:
            src = sum_stat.at[(t // nh) * groups + th // per_group]
            return src, final_stat.at[t // nh, head]
        start = pl.multiple_of((t // nh) * rows + th * small, small)
        return sum_out.at[j, pl.ds(start, small)], final_out.at[t // nh, head, j]

    def final_copy(t, j):
        tx, th = plane(t)
        src, dst = final_refs(t, th, j)
        return pltpu.make_async_remote_copy(
            src_ref=src,
            dst_ref=dst,
            send_sem=final_send.at[j, t],
            recv_sem=final_recv.at[j, t],
            device_id=(patch_of(z, tx, core), th),
            device_id_type=MESH,
        )

    def final_self(j):
        src, dst = final_refs(0, head, j)
        return pltpu.make_async_copy(src, dst, final_recv.at[j, 0])

    def final_start(j):
        final_self(j).start()

        @pl.loop(1, 2 * nh)
        def _(t):
            final_copy(t, j).start()

    for j in range(heads):
        q_start(j)
        if j == 0:
            for load in loads[:2]:
                load.wait()
        loads[2 + 2 * j].wait()
        loads[3 + 2 * j].wait()
        encode(j)

    ones = jnp.ones(values.shape[2:3] + (LANES,), BF16)
    for j in range(heads):
        own_values[j, :, LANES:] = ones
        for chunk in range(nz // 2):
            values[j, chunk, :, LANES:] = ones
        own_keys[j, :rows] = fresh[0, :, j * LANES : (j + 1) * LANES]
        own_values[j, :rows, :LANES] = fresh[1, :, j * LANES : (j + 1) * LANES]
        decode(j, z, 0, 0)
    sum_stat[...] = jnp.zeros(sum_stat.shape, F32)

    for j in range(heads):
        arrive(j, 0)
        q_arrive(j)

    steps = nz // 2
    items = [(s, j) for s in range(steps) for j in range(heads)]

    def arrives_after(k):
        if k < 3 * heads:
            return k - heads
        return k - 2 if k == 3 * heads else k - 1

    for i, (s, j) in enumerate(items):
        if s == 0:
            q_cross(j).wait_recv()
        attend(j, s)
        if s == steps - 1:
            share(j)
            if j == heads - 2:
                for other in range(j):
                    merge(other)
                    final_start(other)
        for k in range(heads, len(items)):
            if arrives_after(k) == i:
                arrive(items[k][1], items[k][0])
    for j in range(max(heads - 2, 0), heads):
        merge(j)
        final_start(j)
    final_start(heads)

    for j in range(heads + 1):
        final_self(j).wait()

    @pl.loop(1, 2 * nh)
    def _(t):
        for j in range(heads + 1):
            final_copy(t, j).wait_recv()

    lane = lax.broadcasted_iota(jnp.int32, (small, LANES), 1)
    row = lax.broadcasted_iota(jnp.int32, (small, LANES), 0)
    mine = lane == row + lax.rem(head, per_group) * small

    def pick(line):
        return jnp.sum(
            jnp.where(mine, jnp.broadcast_to(line, (small, LANES)), 0.0), axis=1, keepdims=True
        )

    @pl.loop(0, nh, unroll=True)
    def _(g):
        shares = share_of(final_stat[0, g], final_stat[1, g])
        for j in range(heads):
            lanes = pl.ds(pl.multiple_of((g * heads + j) * LANES, LANES), LANES)
            results = [final_out[x, g, j].astype(F32) for x in range(2)]
            mixed = mix(results[0], results[1], pick(shares[j : j + 1]))
            out_ref[:, lanes] = mixed.astype(BF16)

    @pl.loop(1, 2 * nh)
    def _(t):
        for j in range(heads):
            q_copy(t, j).wait_send()
        for j in range(heads + 1):
            final_copy(t, j).wait_send()

    for j in range(heads):
        q_cross(j).wait_send()
        for s in range(steps - 1):
            for way in range(2):
                ring_copy(j, s, way).wait_send()
        for way in (fast, slow):

            @pl.when(last_hop(way))
            def _():
                ring_copy(j, steps - 1, way).wait_send()

        for which in range(2):
            part_copy(j, which).wait_send()


def make_local(nz, nh):
    def local(
        queries,
        fresh_keys,
        fresh_values,
        stale_keys,
        stale_values,
        key_basis,
        value_basis,
        owner_table,
        step_counter,
    ):
        heads = key_basis.shape[0]
        rows = fresh_keys.shape[0]
        small = queries.shape[0]
        width = heads * LANES
        seq = stale_keys.shape[0]
        chunks = nz // 2
        groups = rows // LANES
        hbm = pl.BlockSpec(memory_space=pl.ANY)
        vmem = pl.BlockSpec(memory_space=pltpu.VMEM)
        dma = pltpu.SemaphoreType.DMA
        scratch = [
            pltpu.SMEM(owner_table.shape, jnp.int32),
            pltpu.SMEM(step_counter.shape, jnp.int32),
            pltpu.VMEM((2, heads) + key_basis.shape[:0:-1], BF16),
            [pltpu.VMEM((seq // rows, rows, LANES), BF16) for _ in range(2 * heads)],
            pltpu.VMEM((2, rows, width), BF16),
            pltpu.VMEM((heads, LANES, 2 * LANES), BF16),
            pltpu.VMEM((heads, 4 * rows, LANES), BF16),
            pltpu.VMEM((heads, nz, rows, LANES), BF16),
            pltpu.VMEM((heads, chunks, 2 * rows, LANES), BF16),
            pltpu.VMEM((heads, chunks, 2 * rows, 2 * LANES), BF16),
            pltpu.VMEM((heads, 2 * rows, LANES), BF16),
            pltpu.VMEM((heads, 2 * rows, 2 * LANES), BF16),
            pltpu.VMEM((heads, 4 * rows, 2 * LANES), F32),
            pltpu.VMEM((heads, 4 * rows, LANES), F32),
            pltpu.VMEM((heads, 2 * rows, LANES), BF16),
            pltpu.VMEM((heads, 8, LANES), F32),
            pltpu.VMEM((heads, 2 * rows, LANES), BF16),
            pltpu.VMEM((heads, 8, LANES), F32),
            pltpu.VMEM((heads, 2 * rows, LANES), BF16),
            pltpu.VMEM((2 * groups, 8, LANES), F32),
            pltpu.VMEM((2, nh, heads, small, LANES), BF16),
            pltpu.VMEM((2, nh, 8, LANES), F32),
            dma((6 + 2 * heads,)),
            dma((heads, 2 * nh)),
            dma((heads, 2 * nh)),
            dma((2, heads)),
            dma((heads, chunks, 2)),
            dma((heads, chunks, 2)),
            dma((heads, 2)),
            dma((heads, 2)),
            dma((heads + 1, 2 * nh)),
            dma((heads + 1, 2 * nh)),
        ]
        return pl.pallas_call(
            functools.partial(kernel, (heads, nz, nh, rows)),
            out_shape=jax.ShapeDtypeStruct((small, nh * width), BF16),
            in_specs=[hbm] * 9,
            out_specs=vmem,
            scratch_shapes=scratch,
            compiler_params=pltpu.CompilerParams(
                collective_id=0, has_side_effects=True, vmem_limit_bytes=62 << 20
            ),
            name="patch_attention",
        )(
            owner_table,
            step_counter,
            queries,
            fresh_keys,
            fresh_values,
            stale_keys.reshape(seq // rows, rows, width),
            stale_values.reshape(seq // rows, rows, width),
            jnp.swapaxes(key_basis, 1, 2),
            jnp.swapaxes(value_basis, 1, 2),
        )

    return local


def solution(mesh):
    in_specs = (
        P(("patch", "head"), None),
        P("patch", "head"),
        P("patch", "head"),
        P(None, "head"),
        P(None, "head"),
        P("head", None, None),
        P("head", None, None),
        P(),
        P(),
    )
    out_specs = P(("patch", "head"), None)
    local = make_local(mesh.shape["patch"] // 4, mesh.shape["head"])
    return jax.shard_map(local, mesh=mesh, in_specs=in_specs, out_specs=out_specs, check_vma=False)
```
